32 devices in a mesh: dp: 2 (over x), orient: 16 (over z, y, core).
Axes of the slice: x: 2, y: 2, z: 4, core: 2. Of those that a mesh axis runs over, the one named last changes fastest.
Arguments:
- images: bfloat16 [384, 16384], P(('dp', 'orient')), may hold values from -80 to 80
- templates: bfloat16 [4096, 16384], P('orient'), as said below
- index: int32 [4096, 128], P('orient'), may hold values from 0 to 16383
- interp: float32 [4096, 128], P('orient'), may hold values from 0.25 to 1
- inv_noise: float32 [128, 128], replicated, may hold values from 0.5 to 2, as said below
Outputs:
- recon: float32 [16384, 128], P(('dp', 'orient'))
- recon_weight: float32 [16384, 128], P(('dp', 'orient'))
The draws below stay inside these ranges and needn't reach their ends.
Inputs may be any that keep to these rules, and one draw needn't show every extreme that they name: `templates`: every entry has magnitude at most 18 / 128. `inv_noise`: every entry is 0.5, 1 or 2.
All inputs are finite; a program needn't handle non-finite values.
Results may differ from the reference program's by a relative error of at most 0.0029.
Values may be sent and summed in bfloat16 or wider, within the bound.
A program may use at most 128 MiB of HBM per device.

```python
import math
import jax
import jax.numpy as jnp
from jax import lax

PIX = 128
F = 16384
VROWS = 16384
TPL_DEV = 256
NIMG = 384
NTPL = 4096
N_ORIENT = 16


def template_parts(key):
    amp = jnp.exp(jax.random.uniform(jax.random.fold_in(key, 11), (NTPL, 1), jnp.float32, math.log(0.5), math.log(2.0)))
    base = jnp.clip(jax.random.normal(jax.random.fold_in(key, 12), (NTPL, F), jnp.float32), -6.0, 6.0)
    return base * amp * (1.5 / math.sqrt(F))


def draw_templates(key, part):
    values = template_parts(key)
    return values.astype(jnp.bfloat16)


def draw_inv_noise(key, part):
    powers = jax.random.randint(jax.random.fold_in(key, 31), (PIX, PIX), -1, 2)
    return jnp.exp2(powers.astype(jnp.float32))


def draw_images(key, part):
    noise = jnp.clip(jax.random.normal(jax.random.fold_in(key, 21), (NIMG, F), jnp.float32), -6.0, 6.0)
    return noise.astype(jnp.bfloat16)


def touch_ends(array, own_key, least, largest):
    shape = array.shape
    index_at = [jax.random.randint(jax.random.fold_in(own_key, axis), (), 0, shape[axis]) for axis in range(len(shape))]
    array = array.at[tuple(index_at)].set(least)
    longest = shape.index(max(shape))
    index_at[longest] = (index_at[longest] + 1) % shape[longest]
    return array.at[tuple(index_at)].set(largest)


def block_levels(own_key, dims, pieces, low, top_value):
    def one(dim, shards_of):
        heights = jax.random.uniform(jax.random.fold_in(jax.random.fold_in(own_key, 6), dim), (shards_of,), jnp.float32, low / len(pieces), top_value / len(pieces))
        return jnp.repeat(jnp.exp(heights), dims[dim] // shards_of).reshape((-1,) + (1,) * (len(dims) - dim - 1))

    factor_of = one(*pieces[0])
    for cut in pieces[1:]:
        factor_of = factor_of * one(*cut)
    return factor_of


def setup_inputs(seed: int = 0) -> dict:
    seeds = jax.random.split(jax.random.key(seed), 6)
    images = draw_images(jax.random.fold_in(seeds[5], 71), 0)
    templates = draw_templates(jax.random.fold_in(seeds[5], 71), 0)
    index = touch_ends(jax.random.randint(seeds[2], (NTPL, PIX), 0, VROWS), jax.random.fold_in(seeds[2], 1), 0, VROWS - 1).astype(jnp.int32)
    interp = jnp.clip(0.25 + 0.75 * jax.random.uniform(seeds[3], (NTPL, PIX), jnp.float32) ** block_levels(seeds[3], (NTPL, PIX), ((0, 16),), -0.2, 0.2), 0.25, 1.0)
    inv_noise = draw_inv_noise(jax.random.fold_in(seeds[5], 71), 0)
    return dict(images=images, templates=templates, index=index, interp=interp, inv_noise=inv_noise)


def reference(images, templates, index, interp, inv_noise):
    noise_flat = inv_noise.reshape(-1)
    tpl_f = templates.astype(jnp.float32)
    weighted = (tpl_f * noise_flat[None, :]).astype(jnp.bfloat16)
    tnorm = 0.5 * jnp.sum(tpl_f * tpl_f * noise_flat[None, :], axis=1)
    image_f = images.astype(jnp.float32)
    scores = jnp.dot(image_f, weighted.astype(jnp.float32).T) - tnorm[None, :]
    peak = jnp.max(scores, axis=1, keepdims=True)
    expo = jnp.exp(scores - peak)
    posterior = expo / jnp.sum(expo, axis=1, keepdims=True)
    post_b = posterior.astype(jnp.bfloat16)
    mass = jnp.sum(posterior, axis=0)

    def insert(carry, block):
        recon, recw = carry
        start = (block * TPL_DEV).astype(jnp.int32)
        post_blk = lax.dynamic_slice_in_dim(post_b, start, TPL_DEV, 1).astype(jnp.float32)
        sums = jnp.dot(post_blk.T, image_f)
        rows_idx = lax.dynamic_slice_in_dim(index, start, TPL_DEV, 0).reshape(-1)
        weights = lax.dynamic_slice_in_dim(interp, start, TPL_DEV, 0)
        mass_blk = lax.dynamic_slice_in_dim(mass, start, TPL_DEV, 0)
        data_rows = sums.reshape(TPL_DEV * PIX, PIX) * weights.reshape(-1, 1)
        weight_rows = ((weights * mass_blk[:, None])[:, :, None] * inv_noise[None, :, :]).reshape(TPL_DEV * PIX, PIX)
        return (recon.at[rows_idx].add(data_rows), recw.at[rows_idx].add(weight_rows)), None

    init = (jnp.zeros((VROWS, PIX), jnp.float32), jnp.zeros((VROWS, PIX), jnp.float32))
    (recon, recw), unused = lax.scan(insert, init, jnp.arange(N_ORIENT, dtype=jnp.int32))
    return recon, recw
```

```python
import functools

import jax
import jax.numpy as jnp
from jax import lax
from jax.experimental import pallas as pl
from jax.experimental.pallas import tpu as pltpu
from jax.sharding import PartitionSpec as P

LANES = 128
ROWS_STEP = 8
ACCS = 4
UNROLL = 16
VMEM_LIMIT = 56 * 2**20


def data_kernel(post_ref, images_ref, interp_ref, idx_ref, out_ref, rows_ref, *accs):
    step = pl.program_id(0)
    count, side = post_ref.shape[0], out_ref.shape[1]
    volume_rows = out_ref.shape[0]
    every = (out_ref,) + accs

    @pl.when(step == 0)
    def _():
        @pl.loop(0, volume_rows // 64)
        def _(c):
            rows = pl.ds(pl.multiple_of(c * 64, 64), 64)
            for acc in every:
                acc[rows, :] = jnp.zeros((64, side), jnp.float32)

    for j in range(ROWS_STEP):
        block = jnp.dot(
            post_ref[...],
            images_ref[:, j * side : (j + 1) * side],
            preferred_element_type=jnp.float32,
        )
        rows_ref[j * count : (j + 1) * count, :] = block * interp_ref[0, :, j : j + 1]

    @pl.loop(0, ROWS_STEP * count // UNROLL)
    def _(g):
        base = pl.multiple_of(g * UNROLL, UNROLL)
        for k in range(UNROLL):
            acc = every[k % len(every)]
            v = idx_ref[0, 0, base + k]
            acc[pl.ds(v, 1), :] += rows_ref[pl.ds(base + k, 1), :]

    @pl.when(step == pl.num_programs(0) - 1)
    def _():
        @pl.loop(0, volume_rows // 64)
        def _(c):
            rows = pl.ds(pl.multiple_of(c * 64, 64), 64)
            total = every[0][rows, :]
            for acc in accs:
                total = total + acc[rows, :]
            out_ref[rows, :] = total


def insert_data(post, gathered, interp_t, index_t, volume_rows):
    count, images = post.shape
    side = interp_t.shape[0]
    steps = side // ROWS_STEP
    interp_b = interp_t.reshape(steps, ROWS_STEP, count).transpose(0, 2, 1)
    index_b = index_t.reshape(steps, 1, ROWS_STEP * count)
    return pl.pallas_call(
        data_kernel,
        grid=(steps,),
        out_shape=jax.ShapeDtypeStruct((volume_rows, side), jnp.float32),
        in_specs=[
            pl.BlockSpec((count, images), lambda i: (0, 0)),
            pl.BlockSpec((images, ROWS_STEP * side), lambda i: (0, i)),
            pl.BlockSpec((1, count, ROWS_STEP), lambda i: (i, 0, 0)),
            pl.BlockSpec(
                (1, 1, ROWS_STEP * count), lambda i: (i, 0, 0), memory_space=pltpu.SMEM
            ),
        ],
        out_specs=pl.BlockSpec(
            (volume_rows, side), lambda i: (0, 0), pipeline_mode=pl.Buffered(1)
        ),
        scratch_shapes=[pltpu.VMEM((ROWS_STEP * count, side), jnp.float32)]
        + [pltpu.VMEM((volume_rows, side), jnp.float32)] * (ACCS - 1),
        compiler_params=pltpu.CompilerParams(vmem_limit_bytes=VMEM_LIMIT),
        cost_estimate=pl.CostEstimate(
            flops=200_000_000_000, bytes_accessed=200_000_000, transcendentals=0
        ),
    )(post, gathered, interp_b, index_b)


def split(value):
    high = value.astype(jnp.bfloat16)
    return high, (value - high.astype(jnp.float32)).astype(jnp.bfloat16)


def weight_kernel(idx_ref, interp_ref, mass_ref, noise_ref, out_ref, grid_ref):
    step = pl.program_id(0)
    count = idx_ref.shape[1]
    side = noise_ref.shape[0]
    high_rows = out_ref.shape[0] // LANES
    nt = (((1,), (1,)), ((), ()))
    iota_high = lax.broadcasted_iota(jnp.int32, (high_rows, count), 0)
    iota_low = lax.broadcasted_iota(jnp.int32, (LANES, count), 0)
    one, zero = jnp.float32(1), jnp.float32(0)
    for j in range(ROWS_STEP):
        voxel = idx_ref[j : j + 1, :]
        weight = interp_ref[j : j + 1, :] * mass_ref[...]
        w_high = weight.astype(jnp.bfloat16).astype(jnp.float32)
        w_low = weight - w_high
        hot = jnp.where(iota_high == (voxel >> 7), one, zero).astype(jnp.bfloat16)
        low = iota_low == (voxel & (LANES - 1))
        part = lax.dot_general(
            hot,
            jnp.where(low, w_high, zero).astype(jnp.bfloat16),
            nt,
            preferred_element_type=jnp.float32,
        ) + lax.dot_general(
            hot,
            jnp.where(low, w_low, zero).astype(jnp.bfloat16),
            nt,
            preferred_element_type=jnp.float32,
        )
        row = pl.multiple_of((step * ROWS_STEP + j) * high_rows, 8)
        grid_ref[pl.ds(row, high_rows), :] = part

    @pl.when(step == pl.num_programs(0) - 1)
    def _():
        noise = noise_ref[...].astype(jnp.bfloat16)
        tn = (((0,), (0,)), ((), ()))

        @pl.loop(0, high_rows)
        def _(h):
            high, low = split(grid_ref[pl.ds(h, side, stride=high_rows), :])
            out_ref[pl.ds(pl.multiple_of(h * LANES, LANES), LANES), :] = lax.dot_general(
                high, noise, tn, preferred_element_type=jnp.float32
            ) + lax.dot_general(low, noise, tn, preferred_element_type=jnp.float32)


def insert_weights(index_t, interp_t, mass, inv_noise, volume_rows):
    side, count = index_t.shape
    return pl.pallas_call(
        weight_kernel,
        grid=(side // ROWS_STEP,),
        out_shape=jax.ShapeDtypeStruct((volume_rows, side), jnp.float32),
        in_specs=[
            pl.BlockSpec((ROWS_STEP, count), lambda i: (i, 0)),
            pl.BlockSpec((ROWS_STEP, count), lambda i: (i, 0)),
            pl.BlockSpec((1, count), lambda i: (0, 0)),
            pl.BlockSpec((side, side), lambda i: (0, 0)),
        ],
        out_specs=pl.BlockSpec(
            (volume_rows, side), lambda i: (0, 0), pipeline_mode=pl.Buffered(1)
        ),
        scratch_shapes=[pltpu.VMEM((volume_rows, side), jnp.float32)],
        compiler_params=pltpu.CompilerParams(vmem_limit_bytes=VMEM_LIMIT),
        cost_estimate=pl.CostEstimate(
            flops=20_000_000_000, bytes_accessed=20_000_000, transcendentals=0
        ),
    )(index_t, interp_t, mass.reshape(1, count), inv_noise)


def shards(images, templates, index, interp, inv_noise):
    side = inv_noise.shape[0]
    volume_rows = side * side
    noise_flat = inv_noise.reshape(-1)
    index_t, interp_t = index.T, interp.T
    gathered = lax.all_gather(images, "orient", axis=0, tiled=True)
    tpl_f = templates.astype(jnp.float32)
    weighted = (tpl_f * noise_flat[None, :]).astype(jnp.bfloat16)
    tnorm = 0.5 * jnp.sum(tpl_f * tpl_f * noise_flat[None, :], axis=1)
    scores = (
        lax.dot_general(
            weighted, gathered, (((1,), (1,)), ((), ())), preferred_element_type=jnp.float32
        )
        - tnorm[:, None]
    )
    peak_own = jnp.max(scores, axis=0)
    expo = jnp.exp(scores - peak_own[None, :])
    stats = lax.all_gather(jnp.stack([peak_own, jnp.sum(expo, axis=0)]), "orient", axis=0)
    peak = jnp.max(stats[:, 0], axis=0)
    total = jnp.sum(stats[:, 1] * jnp.exp(stats[:, 0] - peak[None, :]), axis=0)
    posterior = expo * (jnp.exp(peak_own - peak) / total)[None, :]
    mass = jnp.sum(posterior, axis=1)
    weight_vol = insert_weights(index_t, interp_t, mass, inv_noise, volume_rows)
    weight_vol, post_b = lax.optimization_barrier(
        (weight_vol, posterior.astype(jnp.bfloat16))
    )
    weight_own = lax.psum_scatter(
        weight_vol, ("dp", "orient"), scatter_dimension=0, tiled=True
    )
    data_vol = insert_data(post_b, gathered, interp_t, index_t, volume_rows)
    data_own = lax.psum_scatter(data_vol, ("dp", "orient"), scatter_dimension=0, tiled=True)
    return data_own, weight_own


def solution(mesh):
    placed = (
        P(("dp", "orient"), None),
        P("orient", None),
        P("orient", None),
        P("orient", None),
        P(),
    )
    return jax.shard_map(
        shards,
        mesh=mesh,
        in_specs=placed,
        out_specs=(P(("dp", "orient"), None), P(("dp", "orient"), None)),
        check_vma=False,
    )
```

```python
import functools

import jax
import jax.numpy as jnp
from jax import lax
from jax.experimental import pallas as pl
from jax.experimental.pallas import tpu as pltpu
from jax.sharding import PartitionSpec as P

LANES = 128
ROWS_STEP = 8
ACCS = 4
UNROLL = 16
LOW_BITS = 5
LOW = 1 << LOW_BITS
VMEM_LIMIT = 56 * 2**20


def data_kernel(post_ref, images_ref, interp_ref, idx_ref, out_ref, rows_ref, *accs):
    step = pl.program_id(0)
    count, side = post_ref.shape[0], out_ref.shape[1]
    volume_rows = out_ref.shape[0]

    @pl.when(step == 0)
    def _():
        @pl.loop(0, volume_rows // 64)
        def _(c):
            rows = pl.ds(pl.multiple_of(c * 64, 64), 64)
            for acc in accs:
                acc[rows, :] = jnp.zeros((64, side), jnp.float32)

    for j in range(ROWS_STEP):
        block = jnp.dot(
            post_ref[...],
            images_ref[:, j * side : (j + 1) * side],
            preferred_element_type=jnp.float32,
        )
        rows_ref[j * count : (j + 1) * count, :] = block * interp_ref[0, :, j : j + 1]

    @pl.loop(0, ROWS_STEP * count // UNROLL)
    def _(g):
        base = pl.multiple_of(g * UNROLL, UNROLL)
        for k in range(UNROLL):
            acc = accs[k % ACCS]
            v = idx_ref[0, 0, base + k]
            acc[pl.ds(v, 1), :] += rows_ref[pl.ds(base + k, 1), :]

    @pl.when(step == pl.num_programs(0) - 1)
    def _():
        @pl.loop(0, volume_rows // 64)
        def _(c):
            rows = pl.ds(pl.multiple_of(c * 64, 64), 64)
            total = accs[0][rows, :]
            for acc in accs[1:]:
                total = total + acc[rows, :]
            out_ref[rows, :] = total.astype(out_ref.dtype)


def insert_data(post, gathered, interp_t, index_t, volume_rows):
    count, images = post.shape
    side = interp_t.shape[0]
    steps = side // ROWS_STEP
    interp_b = interp_t.reshape(steps, ROWS_STEP, count).transpose(0, 2, 1)
    index_b = index_t.reshape(steps, 1, ROWS_STEP * count)
    return pl.pallas_call(
        data_kernel,
        grid=(steps,),
        out_shape=jax.ShapeDtypeStruct((volume_rows, side), jnp.bfloat16),
        in_specs=[
            pl.BlockSpec((count, images), lambda i: (0, 0)),
            pl.BlockSpec((images, ROWS_STEP * side), lambda i: (0, i)),
            pl.BlockSpec((1, count, ROWS_STEP), lambda i: (i, 0, 0)),
            pl.BlockSpec(
                (1, 1, ROWS_STEP * count), lambda i: (i, 0, 0), memory_space=pltpu.SMEM
            ),
        ],
        out_specs=pl.BlockSpec(
            (volume_rows, side), lambda i: (0, 0), pipeline_mode=pl.Buffered(1)
        ),
        scratch_shapes=[pltpu.VMEM((ROWS_STEP * count, side), jnp.float32)]
        + [pltpu.VMEM((volume_rows, side), jnp.float32)] * ACCS,
        compiler_params=pltpu.CompilerParams(vmem_limit_bytes=VMEM_LIMIT),
        cost_estimate=pl.CostEstimate(
            flops=200_000_000_000, bytes_accessed=200_000_000, transcendentals=0
        ),
    )(post, gathered, interp_b, index_b)


def reduce_kernel(
    groups, orient, blocks_ref, out_ref, mine, theirs, landed, own_sem, pair_send, pair_recv, send_sem, recv_sem
):
    half = orient // 2
    chips = groups * half
    group, place = lax.axis_index("dp"), lax.axis_index("orient")
    core = lax.rem(place, 2)
    me = group * half + lax.div(place, 2)
    partner = (group, place + 1 - 2 * core)
    mesh_ids = pl.DeviceIdType.MESH

    def device(chip):
        return (lax.div(chip, half), lax.rem(chip, half) * 2 + core)

    barrier = pltpu.get_barrier_semaphore()
    pl.semaphore_signal(barrier, inc=1, device_id=partner, device_id_type=mesh_ids)

    @pl.loop(1, chips)
    def _(s):
        pl.semaphore_signal(
            barrier,
            inc=1,
            device_id=device(lax.rem(me + s, chips)),
            device_id_type=mesh_ids,
        )

    pl.semaphore_wait(barrier, chips)

    def own_copy(s):
        return pltpu.make_async_copy(
            blocks_ref.at[lax.rem(me + s, chips), core], mine.at[s], own_sem.at[s]
        )

    def pair_copy(s):
        return pltpu.make_async_remote_copy(
            src_ref=blocks_ref.at[lax.rem(me + s, chips), 1 - core],
            dst_ref=theirs.at[s],
            send_sem=pair_send.at[s],
            recv_sem=pair_recv.at[s],
            device_id=partner,
            device_id_type=mesh_ids,
        )

    def chip_copy(s):
        return pltpu.make_async_remote_copy(
            src_ref=mine.at[s],
            dst_ref=landed.at[s],
            send_sem=send_sem.at[s],
            recv_sem=recv_sem.at[s],
            device_id=device(lax.rem(me + s, chips)),
            device_id_type=mesh_ids,
        )

    @pl.loop(1, chips + 1)
    def _(k):
        s = lax.rem(k, chips)
        own_copy(s).start()
        pair_copy(s).start()

    @pl.loop(1, chips)
    def _(s):
        own_copy(s).wait()
        pair_copy(s).wait()
        mine[s] = (mine[s].astype(jnp.float32) + theirs[s].astype(jnp.float32)).astype(
            mine.dtype
        )
        chip_copy(s).start()

    own_copy(0).wait()
    pair_copy(0).wait()
    out_ref[...] = mine[0].astype(jnp.float32) + theirs[0].astype(jnp.float32)

    @pl.loop(1, chips)
    def _(s):
        chip_copy(s).wait()
        out_ref[...] += landed[s].astype(jnp.float32)


def reduce_rows(volume, groups, orient):
    chips = groups * orient // 2
    rows, side = volume.shape[0] // (2 * chips), volume.shape[1]
    return pl.pallas_call(
        functools.partial(reduce_kernel, groups, orient),
        out_shape=jax.ShapeDtypeStruct((rows, side), jnp.float32),
        in_specs=[pl.BlockSpec(memory_space=pl.ANY)],
        out_specs=pl.BlockSpec(memory_space=pltpu.VMEM),
        scratch_shapes=[pltpu.VMEM((chips, rows, side), volume.dtype)] * 3
        + [pltpu.SemaphoreType.DMA((chips,))] * 5,
        compiler_params=pltpu.CompilerParams(
            collective_id=0, has_side_effects=True, vmem_limit_bytes=24 * 2**20
        ),
    )(volume.reshape(chips, 2, rows, side))


def split(value):
    high = value.astype(jnp.bfloat16)
    return high, (value - high.astype(jnp.float32)).astype(jnp.bfloat16)


def weight_kernel(local_ref, weight_ref, noise_ref, out_ref, grid_ref):
    step = pl.program_id(0)
    count = local_ref.shape[1]
    side = noise_ref.shape[0]
    high_rows = grid_ref.shape[0] // side
    nt = (((1,), (1,)), ((), ()))
    iota_high = lax.broadcasted_iota(jnp.int32, (high_rows, count), 0)
    iota_low = lax.broadcasted_iota(jnp.int32, (LOW, count), 0)
    one, zero = jnp.float32(1), jnp.float32(0)
    for j in range(ROWS_STEP):
        local = local_ref[j : j + 1, :]
        hot = jnp.where(iota_high == (local >> LOW_BITS), one, zero)
        low = jnp.where(iota_low == (local & (LOW - 1)), weight_ref[j : j + 1, :], zero)
        part = lax.dot_general(
            hot.astype(jnp.bfloat16),
            low.astype(jnp.bfloat16),
            nt,
            preferred_element_type=jnp.float32,
        )
        row = pl.multiple_of((step * ROWS_STEP + j) * high_rows, 8)
        grid_ref[pl.ds(row, high_rows), :LOW] = part

    @pl.when(step == pl.num_programs(0) - 1)
    def _():
        noise = noise_ref[...].astype(jnp.bfloat16)
        tn = (((0,), (0,)), ((), ()))
        for h in range(out_ref.shape[0] // LOW):
            high, low = split(grid_ref[pl.ds(h, side, stride=high_rows), :])
            block = lax.dot_general(
                high, noise, tn, preferred_element_type=jnp.float32
            ) + lax.dot_general(low, noise, tn, preferred_element_type=jnp.float32)
            out_ref[h * LOW : (h + 1) * LOW, :] = block[:LOW]


def own_weights(local_t, weight_t, inv_noise, rows):
    side, count = local_t.shape
    high_rows = max(8, rows // LOW)
    return pl.pallas_call(
        weight_kernel,
        grid=(side // ROWS_STEP,),
        out_shape=jax.ShapeDtypeStruct((rows, side), jnp.float32),
        in_specs=[
            pl.BlockSpec((ROWS_STEP, count), lambda i: (i, 0)),
            pl.BlockSpec((ROWS_STEP, count), lambda i: (i, 0)),
            pl.BlockSpec((side, side), lambda i: (0, 0)),
        ],
        out_specs=pl.BlockSpec((rows, side), lambda i: (0, 0)),
        scratch_shapes=[pltpu.VMEM((side * high_rows, LANES), jnp.float32)],
        compiler_params=pltpu.CompilerParams(vmem_limit_bytes=24 * 2**20),
        cost_estimate=pl.CostEstimate(
            flops=60_000_000_000, bytes_accessed=20_000_000, transcendentals=0
        ),
    )(local_t, weight_t, inv_noise)


def shards(groups, orient, images, templates, index, interp, inv_noise):
    side = inv_noise.shape[0]
    volume_rows = side * side
    noise_flat = inv_noise.reshape(-1)
    index_t, interp_t = index.T, interp.T
    gathered = lax.all_gather(images, "orient", axis=0, tiled=True)
    places = jnp.concatenate([index.astype(jnp.float32), interp], axis=1)
    gathered, places = lax.optimization_barrier((gathered, places))
    places_all = lax.all_gather(places, "orient", axis=0, tiled=True)
    tpl_f = templates.astype(jnp.float32)
    weighted = (tpl_f * noise_flat[None, :]).astype(jnp.bfloat16)
    tnorm = 0.5 * jnp.sum(tpl_f * tpl_f * noise_flat[None, :], axis=1)
    scores = (
        lax.dot_general(
            weighted, gathered, (((1,), (1,)), ((), ())), preferred_element_type=jnp.float32
        )
        - tnorm[:, None]
    )
    peak_own = jnp.max(scores, axis=0)
    expo = jnp.exp(scores - peak_own[None, :])
    stats = lax.all_gather(jnp.stack([peak_own, jnp.sum(expo, axis=0)]), "orient", axis=0)
    peak = jnp.max(stats[:, 0], axis=0)
    total = jnp.sum(stats[:, 1] * jnp.exp(stats[:, 0] - peak[None, :]), axis=0)
    posterior = expo * (jnp.exp(peak_own - peak) / total)[None, :]
    mass = jnp.sum(posterior, axis=1)
    data_vol = insert_data(
        posterior.astype(jnp.bfloat16), gathered, interp_t, index_t, volume_rows
    )
    rows = volume_rows // (groups * orient)
    first = (lax.axis_index("dp") * orient + lax.axis_index("orient")) * rows
    masses = lax.all_gather(mass, ("dp", "orient"), axis=0)
    mass_all = jnp.sum(masses.reshape(groups, -1), axis=0)
    weight_own = own_weights(
        places_all[:, :side].astype(jnp.int32).T - first,
        places_all[:, side:].T * mass_all[None, :],
        inv_noise,
        rows,
    )
    return reduce_rows(data_vol, groups, orient), weight_own


def solution(mesh):
    placed = (
        P(("dp", "orient"), None),
        P("orient", None),
        P("orient", None),
        P("orient", None),
        P(),
    )
    return jax.shard_map(
        functools.partial(shards, mesh.shape["dp"], mesh.shape["orient"]),
        mesh=mesh,
        in_specs=placed,
        out_specs=(P(("dp", "orient"), None), P(("dp", "orient"), None)),
        check_vma=False,
    )
```

```python
import functools

import jax
import jax.numpy as jnp
from jax import lax
from jax.experimental import pallas as pl
from jax.experimental.pallas import tpu as pltpu
from jax.sharding import PartitionSpec as P

LANES = 128
ROWS_STEP = 8
ACCS = 4
UNROLL = 16
LOW_BITS = 5
LOW = 1 << LOW_BITS
VMEM_LIMIT = 56 * 2**20


def data_kernel(post_ref, images_ref, interp_ref, idx_ref, out_ref, rows_ref, *more):
    accs = (out_ref,) + more
    step = pl.program_id(0)
    count, side = post_ref.shape[0], out_ref.shape[1]
    volume_rows = out_ref.shape[0]

    @pl.when(step == 0)
    def _():
        @pl.loop(0, volume_rows // 64)
        def _(c):
            rows = pl.ds(pl.multiple_of(c * 64, 64), 64)
            for acc in accs:
                acc[rows, :] = jnp.zeros((64, side), jnp.float32)

    for j in range(ROWS_STEP):
        block = jnp.dot(
            post_ref[...],
            images_ref[:, j * side : (j + 1) * side],
            preferred_element_type=jnp.float32,
        )
        rows_ref[j * count : (j + 1) * count, :] = block * interp_ref[0, :, j : j + 1]

    @pl.loop(0, ROWS_STEP * count // UNROLL)
    def _(g):
        base = pl.multiple_of(g * UNROLL, UNROLL)
        for k in range(UNROLL):
            acc = accs[k % ACCS]
            v = idx_ref[0, 0, base + k]
            acc[pl.ds(v, 1), :] += rows_ref[pl.ds(base + k, 1), :]

    @pl.when(step == pl.num_programs(0) - 1)
    def _():
        @pl.loop(0, volume_rows // 64)
        def _(c):
            rows = pl.ds(pl.multiple_of(c * 64, 64), 64)
            total = accs[0][rows, :]
            for acc in accs[1:]:
                total = total + acc[rows, :]
            out_ref[rows, :] = total


def insert_data(post, gathered, interp_t, index_t, volume_rows):
    count, images = post.shape
    side = interp_t.shape[0]
    steps = side // ROWS_STEP
    interp_b = interp_t.reshape(steps, ROWS_STEP, count).transpose(0, 2, 1)
    index_b = index_t.reshape(steps, 1, ROWS_STEP * count)
    return pl.pallas_call(
        data_kernel,
        grid=(steps,),
        out_shape=jax.ShapeDtypeStruct((volume_rows, side), jnp.float32),
        in_specs=[
            pl.BlockSpec((count, images), lambda i: (0, 0)),
            pl.BlockSpec((images, ROWS_STEP * side), lambda i: (0, i)),
            pl.BlockSpec((1, count, ROWS_STEP), lambda i: (i, 0, 0)),
            pl.BlockSpec(
                (1, 1, ROWS_STEP * count), lambda i: (i, 0, 0), memory_space=pltpu.SMEM
            ),
        ],
        out_specs=pl.BlockSpec(
            (volume_rows, side), lambda i: (0, 0), pipeline_mode=pl.Buffered(1)
        ),
        scratch_shapes=[pltpu.VMEM((ROWS_STEP * count, side), jnp.float32)]
        + [pltpu.VMEM((volume_rows, side), jnp.float32)] * (ACCS - 1),
        compiler_params=pltpu.CompilerParams(vmem_limit_bytes=VMEM_LIMIT),
        cost_estimate=pl.CostEstimate(
            flops=200_000_000_000, bytes_accessed=200_000_000, transcendentals=0
        ),
    )(post, gathered, interp_b, index_b)


def reduce_kernel(
    groups,
    orient,
    blocks_ref,
    mass_ref,
    out_ref,
    masses_ref,
    mine,
    theirs,
    ready,
    landed,
    masses,
    own_sem,
    pair_send,
    pair_recv,
    send_sem,
    recv_sem,
    mass_send,
    mass_recv,
):
    half = orient // 2
    chips = groups * half
    group, place = lax.axis_index("dp"), lax.axis_index("orient")
    core = lax.rem(place, 2)
    me = group * half + lax.div(place, 2)
    partner = (group, place + 1 - 2 * core)
    mesh_ids = pl.DeviceIdType.MESH

    def device(chip):
        return (lax.div(chip, half), lax.rem(chip, half) * 2 + core)

    devices = 2 * chips
    rank = group * orient + place

    def ranked(d):
        return (lax.div(d, orient), lax.rem(d, orient))

    barrier = pltpu.get_barrier_semaphore()

    @pl.loop(1, devices)
    def _(s):
        pl.semaphore_signal(
            barrier,
            inc=1,
            device_id=ranked(lax.rem(rank + s, devices)),
            device_id_type=mesh_ids,
        )

    pl.semaphore_wait(barrier, devices - 1)

    def mass_copy(s):
        return pltpu.make_async_remote_copy(
            src_ref=mass_ref,
            dst_ref=masses.at[s],
            send_sem=mass_send.at[s],
            recv_sem=mass_recv.at[s],
            device_id=ranked(lax.rem(rank + s, devices)),
            device_id_type=mesh_ids,
        )

    def own_copy(s):
        return pltpu.make_async_copy(
            blocks_ref.at[lax.rem(me + s, chips), core], mine.at[s], own_sem.at[s]
        )

    def pair_copy(s):
        return pltpu.make_async_remote_copy(
            src_ref=blocks_ref.at[lax.rem(me + s, chips), 1 - core],
            dst_ref=theirs.at[s],
            send_sem=pair_send.at[s],
            recv_sem=pair_recv.at[s],
            device_id=partner,
            device_id_type=mesh_ids,
        )

    def chip_copy(s):
        return pltpu.make_async_remote_copy(
            src_ref=ready.at[s],
            dst_ref=landed.at[s],
            send_sem=send_sem.at[s],
            recv_sem=recv_sem.at[s],
            device_id=device(lax.rem(me + s, chips)),
            device_id_type=mesh_ids,
        )

    @pl.loop(1, chips + 1)
    def _(k):
        s = lax.rem(k, chips)
        own_copy(s).start()
        pair_copy(s).start()

    @pl.loop(1, devices)
    def _(s):
        mass_copy(s).start()

    @pl.loop(1, chips)
    def _(s):
        own_copy(s).wait()
        pair_copy(s).wait()
        ready[s] = (mine[s] + theirs[s]).astype(ready.dtype)
        chip_copy(s).start()

    own_copy(0).wait()
    pair_copy(0).wait()
    out_ref[...] = mine[0] + theirs[0]
    masses_ref[rank] = mass_ref[...]

    @pl.loop(1, devices)
    def _(s):
        mass_copy(s).wait()
        masses_ref[lax.rem(rank + devices - s, devices)] = masses[s]

    @pl.loop(1, chips)
    def _(s):
        chip_copy(s).wait()
        out_ref[...] += landed[s].astype(jnp.float32)


def reduce_rows(volume, mass, groups, orient):
    chips = groups * orient // 2
    rows, side = volume.shape[0] // (2 * chips), volume.shape[1]
    parts = (chips, rows, side)
    mass_rows = mass.reshape(-1, LANES)
    masses = (2 * chips,) + mass_rows.shape
    return pl.pallas_call(
        functools.partial(reduce_kernel, groups, orient),
        out_shape=(
            jax.ShapeDtypeStruct((rows, side), jnp.float32),
            jax.ShapeDtypeStruct(masses, jnp.float32),
        ),
        in_specs=[
            pl.BlockSpec(memory_space=pl.ANY),
            pl.BlockSpec(memory_space=pltpu.VMEM),
        ],
        out_specs=(
            pl.BlockSpec(memory_space=pltpu.VMEM),
            pl.BlockSpec(memory_space=pltpu.VMEM),
        ),
        scratch_shapes=[pltpu.VMEM(parts, jnp.float32)] * 2
        + [pltpu.VMEM(parts, jnp.bfloat16)] * 2
        + [pltpu.VMEM(masses, jnp.float32)]
        + [pltpu.SemaphoreType.DMA((chips,))] * 5
        + [pltpu.SemaphoreType.DMA((2 * chips,))] * 2,
        compiler_params=pltpu.CompilerParams(
            collective_id=0, has_side_effects=True, vmem_limit_bytes=32 * 2**20
        ),
    )(volume.reshape(chips, 2, rows, side), mass_rows)


def split(value):
    high = value.astype(jnp.bfloat16)
    return high, (value - high.astype(jnp.float32)).astype(jnp.bfloat16)


def weight_kernel(local_ref, weight_ref, noise_ref, out_ref, grid_ref):
    step = pl.program_id(0)
    count = local_ref.shape[1]
    side = noise_ref.shape[0]
    high_rows = grid_ref.shape[0] // side
    nt = (((1,), (1,)), ((), ()))
    iota_high = lax.broadcasted_iota(jnp.int32, (high_rows, count), 0)
    iota_low = lax.broadcasted_iota(jnp.int32, (LOW, count), 0)
    one, zero = jnp.float32(1), jnp.float32(0)
    for j in range(ROWS_STEP):
        local = local_ref[j : j + 1, :]
        hot = jnp.where(iota_high == (local >> LOW_BITS), one, zero)
        low = jnp.where(iota_low == (local & (LOW - 1)), weight_ref[j : j + 1, :], zero)
        part = lax.dot_general(
            hot.astype(jnp.bfloat16),
            low.astype(jnp.bfloat16),
            nt,
            preferred_element_type=jnp.float32,
        )
        row = pl.multiple_of((step * ROWS_STEP + j) * high_rows, 8)
        grid_ref[pl.ds(row, high_rows), :LOW] = part

    @pl.when(step == pl.num_programs(0) - 1)
    def _():
        noise = noise_ref[...].astype(jnp.bfloat16)
        tn = (((0,), (0,)), ((), ()))
        for h in range(out_ref.shape[0] // LOW):
            high, low = split(grid_ref[pl.ds(h, side, stride=high_rows), :])
            block = lax.dot_general(
                high, noise, tn, preferred_element_type=jnp.float32
            ) + lax.dot_general(low, noise, tn, preferred_element_type=jnp.float32)
            out_ref[h * LOW : (h + 1) * LOW, :] = block[:LOW]


def own_weights(local_t, weight_t, inv_noise, rows):
    side, count = local_t.shape
    high_rows = max(8, rows // LOW)
    return pl.pallas_call(
        weight_kernel,
        grid=(side // ROWS_STEP,),
        out_shape=jax.ShapeDtypeStruct((rows, side), jnp.float32),
        in_specs=[
            pl.BlockSpec((ROWS_STEP, count), lambda i: (i, 0)),
            pl.BlockSpec((ROWS_STEP, count), lambda i: (i, 0)),
            pl.BlockSpec((side, side), lambda i: (0, 0)),
        ],
        out_specs=pl.BlockSpec((rows, side), lambda i: (0, 0)),
        scratch_shapes=[pltpu.VMEM((side * high_rows, LANES), jnp.float32)],
        compiler_params=pltpu.CompilerParams(vmem_limit_bytes=24 * 2**20),
        cost_estimate=pl.CostEstimate(
            flops=60_000_000_000, bytes_accessed=20_000_000, transcendentals=0
        ),
    )(local_t, weight_t, inv_noise)


def shards(groups, orient, images, templates, index, interp, inv_noise):
    side = inv_noise.shape[0]
    volume_rows = side * side
    noise_flat = inv_noise.reshape(-1)
    index_t, interp_t = index.T, interp.T
    gathered = lax.all_gather(images, "orient", axis=0, tiled=True)
    places = jnp.concatenate([index.astype(jnp.float32), interp], axis=1)
    gathered, places = lax.optimization_barrier((gathered, places))
    places_all = lax.all_gather(places, "orient", axis=0, tiled=True)
    tpl_f = templates.astype(jnp.float32)
    weighted = (tpl_f * noise_flat[None, :]).astype(jnp.bfloat16)
    tnorm = 0.5 * jnp.sum(tpl_f * tpl_f * noise_flat[None, :], axis=1)
    scores = (
        lax.dot_general(
            weighted, gathered, (((1,), (1,)), ((), ())), preferred_element_type=jnp.float32
        )
        - tnorm[:, None]
    )
    peak_own = jnp.max(scores, axis=0)
    expo = jnp.exp(scores - peak_own[None, :])
    stats = lax.all_gather(jnp.stack([peak_own, jnp.sum(expo, axis=0)]), "orient", axis=0)
    peak = jnp.max(stats[:, 0], axis=0)
    total = jnp.sum(stats[:, 1] * jnp.exp(stats[:, 0] - peak[None, :]), axis=0)
    posterior = expo * (jnp.exp(peak_own - peak) / total)[None, :]
    mass = jnp.sum(posterior, axis=1)
    data_vol = insert_data(
        posterior.astype(jnp.bfloat16), gathered, interp_t, index_t, volume_rows
    )
    rows = volume_rows // (groups * orient)
    first = (lax.axis_index("dp") * orient + lax.axis_index("orient")) * rows
    data_own, masses = reduce_rows(data_vol, mass, groups, orient)
    mass_all = jnp.sum(masses.reshape(groups, -1), axis=0)
    weight_own = own_weights(
        places_all[:, :side].astype(jnp.int32).T - first,
        places_all[:, side:].T * mass_all[None, :],
        inv_noise,
        rows,
    )
    return data_own, weight_own


def solution(mesh):
    placed = (
        P(("dp", "orient"), None),
        P("orient", None),
        P("orient", None),
        P("orient", None),
        P(),
    )
    return jax.shard_map(
        functools.partial(shards, mesh.shape["dp"], mesh.shape["orient"]),
        mesh=mesh,
        in_specs=placed,
        out_specs=(P(("dp", "orient"), None), P(("dp", "orient"), None)),
        check_vma=False,
    )
```

```python
import functools

import jax
import jax.numpy as jnp
from jax import lax
from jax.experimental import pallas as pl
from jax.experimental.pallas import tpu as pltpu
from jax.sharding import PartitionSpec as P

LANES = 128
ROWS_STEP = 8
ACCS = 4
UNROLL = 16
LOW_BITS = 5
LOW = 1 << LOW_BITS
VMEM_LIMIT = 56 * 2**20


def data_kernel(post_ref, images_ref, interp_ref, idx_ref, out_ref, rows_ref, *more):
    accs = (out_ref,) + more
    step = pl.program_id(0)
    count, side = post_ref.shape[0], out_ref.shape[1]
    volume_rows = out_ref.shape[0]

    @pl.when(step == 0)
    def _():
        @pl.loop(0, volume_rows // 64)
        def _(c):
            rows = pl.ds(pl.multiple_of(c * 64, 64), 64)
            for acc in accs:
                acc[rows, :] = jnp.zeros((64, side), jnp.float32)

    for j in range(ROWS_STEP):
        block = jnp.dot(
            post_ref[...],
            images_ref[:, j * side : (j + 1) * side],
            preferred_element_type=jnp.float32,
        )
        rows_ref[j * count : (j + 1) * count, :] = block * interp_ref[0, :, j : j + 1]

    @pl.loop(0, ROWS_STEP * count // UNROLL)
    def _(g):
        base = pl.multiple_of(g * UNROLL, UNROLL)
        for k in range(0, UNROLL, ACCS):
            voxels = [idx_ref[0, 0, base + k + a] for a in range(ACCS)]
            summed = [
                accs[a][pl.ds(voxels[a], 1), :] + rows_ref[pl.ds(base + k + a, 1), :]
                for a in range(ACCS)
            ]
            for a in range(ACCS):
                accs[a][pl.ds(voxels[a], 1), :] = summed[a]

    @pl.when(step == pl.num_programs(0) - 1)
    def _():
        @pl.loop(0, volume_rows // 64)
        def _(c):
            rows = pl.ds(pl.multiple_of(c * 64, 64), 64)
            total = accs[0][rows, :]
            for acc in accs[1:]:
                total = total + acc[rows, :]
            out_ref[rows, :] = total


def insert_data(post, gathered, interp_t, index_t, volume_rows):
    count, images = post.shape
    side = interp_t.shape[0]
    steps = side // ROWS_STEP
    interp_b = interp_t.reshape(steps, ROWS_STEP, count).transpose(0, 2, 1)
    index_b = index_t.reshape(steps, 1, ROWS_STEP * count)
    return pl.pallas_call(
        data_kernel,
        grid=(steps,),
        out_shape=jax.ShapeDtypeStruct((volume_rows, side), jnp.float32),
        in_specs=[
            pl.BlockSpec((count, images), lambda i: (0, 0)),
            pl.BlockSpec((images, ROWS_STEP * side), lambda i: (0, i)),
            pl.BlockSpec((1, count, ROWS_STEP), lambda i: (i, 0, 0)),
            pl.BlockSpec(
                (1, 1, ROWS_STEP * count), lambda i: (i, 0, 0), memory_space=pltpu.SMEM
            ),
        ],
        out_specs=pl.BlockSpec(
            (volume_rows, side), lambda i: (0, 0), pipeline_mode=pl.Buffered(1)
        ),
        scratch_shapes=[pltpu.VMEM((ROWS_STEP * count, side), jnp.float32)]
        + [pltpu.VMEM((volume_rows, side), jnp.float32)] * (ACCS - 1),
        compiler_params=pltpu.CompilerParams(vmem_limit_bytes=VMEM_LIMIT),
        cost_estimate=pl.CostEstimate(
            flops=200_000_000_000, bytes_accessed=200_000_000, transcendentals=0
        ),
    )(post, gathered, interp_b, index_b)


def reduce_kernel(
    groups,
    orient,
    blocks_ref,
    mass_ref,
    out_ref,
    masses_ref,
    mine,
    theirs,
    ready,
    landed,
    masses,
    own_sem,
    pair_send,
    pair_recv,
    send_sem,
    recv_sem,
    mass_send,
    mass_recv,
):
    half = orient // 2
    chips = groups * half
    group, place = lax.axis_index("dp"), lax.axis_index("orient")
    core = lax.rem(place, 2)
    me = group * half + lax.div(place, 2)
    partner = (group, place + 1 - 2 * core)
    mesh_ids = pl.DeviceIdType.MESH

    def device(chip):
        return (lax.div(chip, half), lax.rem(chip, half) * 2 + core)

    devices = 2 * chips
    rank = group * orient + place

    def ranked(d):
        return (lax.div(d, orient), lax.rem(d, orient))

    barrier = pltpu.get_barrier_semaphore()

    @pl.loop(1, devices)
    def _(s):
        pl.semaphore_signal(
            barrier,
            inc=1,
            device_id=ranked(lax.rem(rank + s, devices)),
            device_id_type=mesh_ids,
        )

    pl.semaphore_wait(barrier, devices - 1)

    def mass_copy(s):
        return pltpu.make_async_remote_copy(
            src_ref=mass_ref,
            dst_ref=masses.at[s],
            send_sem=mass_send.at[s],
            recv_sem=mass_recv.at[s],
            device_id=ranked(lax.rem(rank + s, devices)),
            device_id_type=mesh_ids,
        )

    def own_copy(s):
        return pltpu.make_async_copy(
            blocks_ref.at[lax.rem(me + s, chips), core], mine.at[s], own_sem.at[s]
        )

    def pair_copy(s):
        return pltpu.make_async_remote_copy(
            src_ref=blocks_ref.at[lax.rem(me + s, chips), 1 - core],
            dst_ref=theirs.at[s],
            send_sem=pair_send.at[s],
            recv_sem=pair_recv.at[s],
            device_id=partner,
            device_id_type=mesh_ids,
        )

    def chip_copy(s):
        return pltpu.make_async_remote_copy(
            src_ref=ready.at[s],
            dst_ref=landed.at[s],
            send_sem=send_sem.at[s],
            recv_sem=recv_sem.at[s],
            device_id=device(lax.rem(me + s, chips)),
            device_id_type=mesh_ids,
        )

    @pl.loop(1, chips + 1)
    def _(k):
        s = lax.rem(k, chips)
        own_copy(s).start()
        pair_copy(s).start()

    @pl.loop(1, devices)
    def _(s):
        mass_copy(s).start()

    @pl.loop(1, chips)
    def _(s):
        own_copy(s).wait()
        pair_copy(s).wait()
        ready[s] = (mine[s] + theirs[s]).astype(ready.dtype)
        chip_copy(s).start()

    own_copy(0).wait()
    pair_copy(0).wait()
    out_ref[...] = mine[0] + theirs[0]
    masses_ref[rank] = mass_ref[...]

    @pl.loop(1, devices)
    def _(s):
        mass_copy(s).wait()
        masses_ref[lax.rem(rank + devices - s, devices)] = masses[s]

    @pl.loop(1, chips)
    def _(s):
        chip_copy(s).wait()
        out_ref[...] += landed[s].astype(jnp.float32)


def reduce_rows(volume, mass, groups, orient):
    chips = groups * orient // 2
    rows, side = volume.shape[0] // (2 * chips), volume.shape[1]
    parts = (chips, rows, side)
    mass_rows = mass.reshape(-1, LANES)
    masses = (2 * chips,) + mass_rows.shape
    return pl.pallas_call(
        functools.partial(reduce_kernel, groups, orient),
        out_shape=(
            jax.ShapeDtypeStruct((rows, side), jnp.float32),
            jax.ShapeDtypeStruct(masses, jnp.float32),
        ),
        in_specs=[
            pl.BlockSpec(memory_space=pl.ANY),
            pl.BlockSpec(memory_space=pltpu.VMEM),
        ],
        out_specs=(
            pl.BlockSpec(memory_space=pltpu.VMEM),
            pl.BlockSpec(memory_space=pltpu.VMEM),
        ),
        scratch_shapes=[pltpu.VMEM(parts, jnp.float32)] * 2
        + [pltpu.VMEM(parts, jnp.bfloat16)] * 2
        + [pltpu.VMEM(masses, jnp.float32)]
        + [pltpu.SemaphoreType.DMA((chips,))] * 5
        + [pltpu.SemaphoreType.DMA((2 * chips,))] * 2,
        compiler_params=pltpu.CompilerParams(
            collective_id=0, has_side_effects=True, vmem_limit_bytes=VMEM_LIMIT
        ),
    )(volume.reshape(chips, 2, rows, side), mass_rows)


def split(value):
    high = value.astype(jnp.bfloat16)
    return high, (value - high.astype(jnp.float32)).astype(jnp.bfloat16)


def weight_kernel(local_ref, weight_ref, noise_ref, out_ref, grid_ref):
    step = pl.program_id(0)
    count = local_ref.shape[1]
    side = noise_ref.shape[0]
    high_rows = grid_ref.shape[0] // side
    nt = (((1,), (1,)), ((), ()))
    iota_high = lax.broadcasted_iota(jnp.int32, (high_rows, count), 0)
    iota_low = lax.broadcasted_iota(jnp.int32, (LOW, count), 0)
    one, zero = jnp.float32(1), jnp.float32(0)
    for j in range(ROWS_STEP):
        local = local_ref[j : j + 1, :]
        hot = jnp.where(iota_high == (local >> LOW_BITS), one, zero)
        low = jnp.where(iota_low == (local & (LOW - 1)), weight_ref[j : j + 1, :], zero)
        part = lax.dot_general(
            hot.astype(jnp.bfloat16),
            low.astype(jnp.bfloat16),
            nt,
            preferred_element_type=jnp.float32,
        )
        row = pl.multiple_of((step * ROWS_STEP + j) * high_rows, 8)
        grid_ref[pl.ds(row, high_rows), :LOW] = part

    @pl.when(step == pl.num_programs(0) - 1)
    def _():
        noise = noise_ref[...].astype(jnp.bfloat16)
        tn = (((0,), (0,)), ((), ()))
        for h in range(out_ref.shape[0] // LOW):
            high, low = split(grid_ref[pl.ds(h, side, stride=high_rows), :])
            block = lax.dot_general(
                high, noise, tn, preferred_element_type=jnp.float32
            ) + lax.dot_general(low, noise, tn, preferred_element_type=jnp.float32)
            out_ref[h * LOW : (h + 1) * LOW, :] = block[:LOW]


def own_weights(local_t, weight_t, inv_noise, rows):
    side, count = local_t.shape
    high_rows = max(8, rows // LOW)
    return pl.pallas_call(
        weight_kernel,
        grid=(side // ROWS_STEP,),
        out_shape=jax.ShapeDtypeStruct((rows, side), jnp.float32),
        in_specs=[
            pl.BlockSpec((ROWS_STEP, count), lambda i: (i, 0)),
            pl.BlockSpec((ROWS_STEP, count), lambda i: (i, 0)),
            pl.BlockSpec((side, side), lambda i: (0, 0)),
        ],
        out_specs=pl.BlockSpec((rows, side), lambda i: (0, 0)),
        scratch_shapes=[pltpu.VMEM((side * high_rows, LANES), jnp.float32)],
        compiler_params=pltpu.CompilerParams(vmem_limit_bytes=24 * 2**20),
        cost_estimate=pl.CostEstimate(
            flops=60_000_000_000, bytes_accessed=20_000_000, transcendentals=0
        ),
    )(local_t, weight_t, inv_noise)


def stats_kernel(orient, own_ref, out_ref, landed, send_sem, recv_sem):
    group, place = lax.axis_index("dp"), lax.axis_index("orient")
    mesh_ids = pl.DeviceIdType.MESH
    barrier = pltpu.get_barrier_semaphore()

    @pl.loop(1, orient)
    def _(s):
        pl.semaphore_signal(
            barrier,
            inc=1,
            device_id=(group, lax.rem(place + s, orient)),
            device_id_type=mesh_ids,
        )

    pl.semaphore_wait(barrier, orient - 1)

    def copy(s):
        return pltpu.make_async_remote_copy(
            src_ref=own_ref,
            dst_ref=landed.at[s],
            send_sem=send_sem.at[s],
            recv_sem=recv_sem.at[s],
            device_id=(group, lax.rem(place + s, orient)),
            device_id_type=mesh_ids,
        )

    @pl.loop(1, orient)
    def _(s):
        copy(s).start()

    out_ref[place] = own_ref[...]

    @pl.loop(1, orient)
    def _(s):
        copy(s).wait()
        out_ref[lax.rem(place + orient - s, orient)] = landed[s]


def gather_stats(own, orient):
    count = own.shape[1]
    pad = -count % (8 * LANES)
    rows = jnp.pad(own, ((0, 0), (0, pad))).reshape(-1, LANES)
    stats = pl.pallas_call(
        functools.partial(stats_kernel, orient),
        out_shape=jax.ShapeDtypeStruct((orient,) + rows.shape, jnp.float32),
        in_specs=[pl.BlockSpec(memory_space=pltpu.VMEM)],
        out_specs=pl.BlockSpec(memory_space=pltpu.VMEM),
        scratch_shapes=[pltpu.VMEM((orient,) + rows.shape, jnp.float32)]
        + [pltpu.SemaphoreType.DMA((orient,))] * 2,
        compiler_params=pltpu.CompilerParams(
            collective_id=1, has_side_effects=True, vmem_limit_bytes=16 * 2**20
        ),
    )(rows)
    return stats.reshape(orient, 2, -1)[:, :, :count]


def shards(groups, orient, images, templates, index, interp, inv_noise):
    side = inv_noise.shape[0]
    volume_rows = side * side
    noise_flat = inv_noise.reshape(-1)
    index_t, interp_t = index.T, interp.T
    gathered = lax.all_gather(images, "orient", axis=0, tiled=True)
    places = jnp.concatenate([index.astype(jnp.float32), interp], axis=1)
    gathered, places = lax.optimization_barrier((gathered, places))
    places_all = lax.all_gather(places, "orient", axis=0, tiled=True)
    tpl_f = templates.astype(jnp.float32)
    weighted = (tpl_f * noise_flat[None, :]).astype(jnp.bfloat16)
    tnorm = 0.5 * jnp.sum(tpl_f * tpl_f * noise_flat[None, :], axis=1)
    scores = (
        lax.dot_general(
            weighted, gathered, (((1,), (1,)), ((), ())), preferred_element_type=jnp.float32
        )
        - tnorm[:, None]
    )
    peak_own = jnp.max(scores, axis=0)
    expo = jnp.exp(scores - peak_own[None, :])
    stats = gather_stats(jnp.stack([peak_own, jnp.sum(expo, axis=0)]), orient)
    peak = jnp.max(stats[:, 0], axis=0)
    total = jnp.sum(stats[:, 1] * jnp.exp(stats[:, 0] - peak[None, :]), axis=0)
    posterior = expo * (jnp.exp(peak_own - peak) / total)[None, :]
    mass = jnp.sum(posterior, axis=1)
    data_vol = insert_data(
        posterior.astype(jnp.bfloat16), gathered, interp_t, index_t, volume_rows
    )
    rows = volume_rows // (groups * orient)
    first = (lax.axis_index("dp") * orient + lax.axis_index("orient")) * rows
    data_own, masses = reduce_rows(data_vol, mass, groups, orient)
    mass_all = jnp.sum(masses.reshape(groups, -1), axis=0)
    weight_own = own_weights(
        places_all[:, :side].astype(jnp.int32).T - first,
        places_all[:, side:].T * mass_all[None, :],
        inv_noise,
        rows,
    )
    return data_own, weight_own


def solution(mesh):
    placed = (
        P(("dp", "orient"), None),
        P("orient", None),
        P("orient", None),
        P("orient", None),
        P(),
    )
    return jax.shard_map(
        functools.partial(shards, mesh.shape["dp"], mesh.shape["orient"]),
        mesh=mesh,
        in_specs=placed,
        out_specs=(P(("dp", "orient"), None), P(("dp", "orient"), None)),
        check_vma=False,
    )
```

```python
import functools

import jax
import jax.numpy as jnp
from jax import lax
from jax.experimental import pallas as pl
from jax.experimental.pallas import tpu as pltpu
from jax.sharding import PartitionSpec as P

LANES = 128
ROWS_STEP = 8
ACCS = 4
UNROLL = 16
LOW_BITS = 5
LOW = 1 << LOW_BITS
VMEM_LIMIT = 56 * 2**20


def data_kernel(post_ref, images_ref, interp_ref, idx_ref, out_ref, rows_ref, *more):
    accs = (out_ref,) + more
    step = pl.program_id(0)
    count, side = post_ref.shape[0], out_ref.shape[1]
    volume_rows = out_ref.shape[0]

    @pl.when(step == 0)
    def _():
        @pl.loop(0, volume_rows // 64)
        def _(c):
            rows = pl.ds(pl.multiple_of(c * 64, 64), 64)
            for acc in accs:
                acc[rows, :] = jnp.zeros((64, side), jnp.float32)

    for j in range(ROWS_STEP):
        block = jnp.dot(
            post_ref[...],
            images_ref[:, j * side : (j + 1) * side],
            preferred_element_type=jnp.float32,
        )
        rows_ref[j * count : (j + 1) * count, :] = block * interp_ref[0, :, j : j + 1]

    @pl.loop(0, ROWS_STEP * count // UNROLL)
    def _(g):
        base = pl.multiple_of(g * UNROLL, UNROLL)
        for k in range(0, UNROLL, ACCS):
            voxels = [idx_ref[0, 0, base + k + a] for a in range(ACCS)]
            summed = [
                accs[a][pl.ds(voxels[a], 1), :] + rows_ref[pl.ds(base + k + a, 1), :]
                for a in range(ACCS)
            ]
            for a in range(ACCS):
                accs[a][pl.ds(voxels[a], 1), :] = summed[a]

    @pl.when(step == pl.num_programs(0) - 1)
    def _():
        @pl.loop(0, volume_rows // 64)
        def _(c):
            rows = pl.ds(pl.multiple_of(c * 64, 64), 64)
            total = accs[0][rows, :]
            for acc in accs[1:]:
                total = total + acc[rows, :]
            out_ref[rows, :] = total


def insert_data(post, gathered, interp_t, index_t, volume_rows):
    count, images = post.shape
    side = interp_t.shape[0]
    steps = side // ROWS_STEP
    interp_b = interp_t.reshape(steps, ROWS_STEP, count).transpose(0, 2, 1)
    index_b = index_t.reshape(steps, 1, ROWS_STEP * count)
    return pl.pallas_call(
        data_kernel,
        grid=(steps,),
        out_shape=jax.ShapeDtypeStruct((volume_rows, side), jnp.float32),
        in_specs=[
            pl.BlockSpec((count, images), lambda i: (0, 0)),
            pl.BlockSpec((images, ROWS_STEP * side), lambda i: (0, i)),
            pl.BlockSpec((1, count, ROWS_STEP), lambda i: (i, 0, 0)),
            pl.BlockSpec(
                (1, 1, ROWS_STEP * count), lambda i: (i, 0, 0), memory_space=pltpu.SMEM
            ),
        ],
        out_specs=pl.BlockSpec(
            (volume_rows, side), lambda i: (0, 0), pipeline_mode=pl.Buffered(1)
        ),
        scratch_shapes=[pltpu.VMEM((ROWS_STEP * count, side), jnp.float32)]
        + [pltpu.VMEM((volume_rows, side), jnp.float32)] * (ACCS - 1),
        compiler_params=pltpu.CompilerParams(vmem_limit_bytes=VMEM_LIMIT),
        cost_estimate=pl.CostEstimate(
            flops=200_000_000_000, bytes_accessed=200_000_000, transcendentals=0
        ),
    )(post, gathered, interp_b, index_b)


def reduce_kernel(
    groups,
    orient,
    blocks_ref,
    mass_ref,
    local_ref,
    interp_ref,
    noise_ref,
    out_ref,
    weight_ref,
    grid_ref,
    mass_row,
    mine,
    theirs,
    ready,
    landed,
    masses,
    own_sem,
    pair_send,
    pair_recv,
    send_sem,
    recv_sem,
    mass_send,
    mass_recv,
):
    half = orient // 2
    chips = groups * half
    group, place = lax.axis_index("dp"), lax.axis_index("orient")
    core = lax.rem(place, 2)
    me = group * half + lax.div(place, 2)
    partner = (group, place + 1 - 2 * core)
    mesh_ids = pl.DeviceIdType.MESH

    def device(chip):
        return (lax.div(chip, half), lax.rem(chip, half) * 2 + core)

    devices = 2 * chips
    rank = group * orient + place

    def ranked(d):
        return (lax.div(d, orient), lax.rem(d, orient))

    barrier = pltpu.get_barrier_semaphore()

    @pl.loop(1, devices)
    def _(s):
        pl.semaphore_signal(
            barrier,
            inc=1,
            device_id=ranked(lax.rem(rank + s, devices)),
            device_id_type=mesh_ids,
        )

    pl.semaphore_wait(barrier, devices - 1)

    def mass_copy(s):
        return pltpu.make_async_remote_copy(
            src_ref=mass_ref,
            dst_ref=masses.at[s],
            send_sem=mass_send.at[s],
            recv_sem=mass_recv.at[s],
            device_id=ranked(lax.rem(rank + s, devices)),
            device_id_type=mesh_ids,
        )

    def own_copy(s):
        return pltpu.make_async_copy(
            blocks_ref.at[lax.rem(me + s, chips), core], mine.at[s], own_sem.at[s]
        )

    def pair_copy(s):
        return pltpu.make_async_remote_copy(
            src_ref=blocks_ref.at[lax.rem(me + s, chips), 1 - core],
            dst_ref=theirs.at[s],
            send_sem=pair_send.at[s],
            recv_sem=pair_recv.at[s],
            device_id=partner,
            device_id_type=mesh_ids,
        )

    def chip_copy(s):
        return pltpu.make_async_remote_copy(
            src_ref=ready.at[s],
            dst_ref=landed.at[s],
            send_sem=send_sem.at[s],
            recv_sem=recv_sem.at[s],
            device_id=device(lax.rem(me + s, chips)),
            device_id_type=mesh_ids,
        )

    @pl.loop(1, devices)
    def _(s):
        mass_copy(s).start()

    @pl.loop(1, chips + 1)
    def _(k):
        s = lax.rem(k, chips)
        own_copy(s).start()
        pair_copy(s).start()

    @pl.loop(1, chips)
    def _(s):
        own_copy(s).wait()
        pair_copy(s).wait()
        ready[s] = (mine[s] + theirs[s]).astype(ready.dtype)
        chip_copy(s).start()

    own_copy(0).wait()
    pair_copy(0).wait()
    out_ref[...] = mine[0] + theirs[0]
    mass_row[...] = jnp.zeros_like(mass_row)
    mass_rows = mass_ref.shape[0]

    def add_mass(d, ref):
        start = lax.rem(d, orient) * (mass_rows * LANES)
        for k in range(mass_rows):
            lanes = pl.ds(pl.multiple_of(start + k * LANES, LANES), LANES)
            mass_row[:, lanes] += ref[k : k + 1, :]

    add_mass(rank, mass_ref)

    @pl.loop(1, devices)
    def _(s):
        mass_copy(s).wait()
        add_mass(lax.rem(rank + devices - s, devices), masses.at[s])

    insert_weights(local_ref, interp_ref, mass_row, noise_ref, weight_ref, grid_ref)

    @pl.loop(1, chips)
    def _(s):
        chip_copy(s).wait()
        out_ref[...] += landed[s].astype(jnp.float32)


def reduce_rows(volume, mass, local_t, interp_t, inv_noise, groups, orient):
    chips = groups * orient // 2
    rows, side = volume.shape[0] // (2 * chips), volume.shape[1]
    parts = (chips, rows, side)
    mass_rows = mass.reshape(-1, LANES)
    masses = (2 * chips,) + mass_rows.shape
    return pl.pallas_call(
        functools.partial(reduce_kernel, groups, orient),
        out_shape=(
            jax.ShapeDtypeStruct((rows, side), jnp.float32),
            jax.ShapeDtypeStruct((rows, side), jnp.float32),
        ),
        in_specs=[pl.BlockSpec(memory_space=pl.ANY)]
        + [pl.BlockSpec(memory_space=pltpu.VMEM)] * 4,
        out_specs=(
            pl.BlockSpec(memory_space=pltpu.VMEM),
            pl.BlockSpec(memory_space=pltpu.VMEM),
        ),
        scratch_shapes=[
            pltpu.VMEM((side * max(8, rows // LOW), LANES), jnp.float32),
            pltpu.VMEM((1, local_t.shape[1]), jnp.float32),
        ]
        + [pltpu.VMEM(parts, jnp.float32)] * 2
        + [pltpu.VMEM(parts, jnp.bfloat16)] * 2
        + [pltpu.VMEM(masses, jnp.float32)]
        + [pltpu.SemaphoreType.DMA((chips,))] * 5
        + [pltpu.SemaphoreType.DMA((2 * chips,))] * 2,
        compiler_params=pltpu.CompilerParams(
            collective_id=0, has_side_effects=True, vmem_limit_bytes=VMEM_LIMIT
        ),
    )(volume.reshape(chips, 2, rows, side), mass_rows, local_t, interp_t, inv_noise)


def split(value):
    high = value.astype(jnp.bfloat16)
    return high, (value - high.astype(jnp.float32)).astype(jnp.bfloat16)


def insert_weights(local_ref, interp_ref, mass_row, noise_ref, out_ref, grid_ref):
    count = local_ref.shape[1]
    side = noise_ref.shape[0]
    high_rows = grid_ref.shape[0] // side
    nt = (((1,), (1,)), ((), ()))
    tn = (((0,), (0,)), ((), ()))
    one, zero = jnp.float32(1), jnp.float32(0)

    @pl.loop(0, side // ROWS_STEP)
    def _(step):
        iota_high = lax.broadcasted_iota(jnp.int32, (high_rows, count), 0)
        iota_low = lax.broadcasted_iota(jnp.int32, (LOW, count), 0)
        block = pl.ds(pl.multiple_of(step * ROWS_STEP, ROWS_STEP), ROWS_STEP)
        locals_, weights = local_ref[block, :], interp_ref[block, :] * mass_row[...]
        for j in range(ROWS_STEP):
            local = locals_[j : j + 1, :]
            hot = jnp.where(iota_high == (local >> LOW_BITS), one, zero)
            low = jnp.where(iota_low == (local & (LOW - 1)), weights[j : j + 1, :], zero)
            part = lax.dot_general(
                hot.astype(jnp.bfloat16),
                low.astype(jnp.bfloat16),
                nt,
                preferred_element_type=jnp.float32,
            )
            row = pl.multiple_of((step * ROWS_STEP + j) * high_rows, 8)
            grid_ref[pl.ds(row, high_rows), :LOW] = part

    noise = noise_ref[...].astype(jnp.bfloat16)
    for h in range(out_ref.shape[0] // LOW):
        high, low = split(grid_ref[pl.ds(h, side, stride=high_rows), :])
        block = lax.dot_general(
            high, noise, tn, preferred_element_type=jnp.float32
        ) + lax.dot_general(low, noise, tn, preferred_element_type=jnp.float32)
        out_ref[h * LOW : (h + 1) * LOW, :] = block[:LOW]


def stats_kernel(orient, own_ref, out_ref, landed, send_sem, recv_sem):
    group, place = lax.axis_index("dp"), lax.axis_index("orient")
    mesh_ids = pl.DeviceIdType.MESH
    barrier = pltpu.get_barrier_semaphore()

    @pl.loop(1, orient)
    def _(s):
        pl.semaphore_signal(
            barrier,
            inc=1,
            device_id=(group, lax.rem(place + s, orient)),
            device_id_type=mesh_ids,
        )

    pl.semaphore_wait(barrier, orient - 1)

    def copy(s):
        return pltpu.make_async_remote_copy(
            src_ref=own_ref,
            dst_ref=landed.at[s],
            send_sem=send_sem.at[s],
            recv_sem=recv_sem.at[s],
            device_id=(group, lax.rem(place + s, orient)),
            device_id_type=mesh_ids,
        )

    @pl.loop(1, orient)
    def _(s):
        copy(s).start()

    out_ref[place] = own_ref[...]

    @pl.loop(1, orient)
    def _(s):
        copy(s).wait()
        out_ref[lax.rem(place + orient - s, orient)] = landed[s]


def gather_stats(own, orient):
    count = own.shape[1]
    pad = -count % (8 * LANES)
    rows = jnp.pad(own, ((0, 0), (0, pad))).reshape(-1, LANES)
    stats = pl.pallas_call(
        functools.partial(stats_kernel, orient),
        out_shape=jax.ShapeDtypeStruct((orient,) + rows.shape, jnp.float32),
        in_specs=[pl.BlockSpec(memory_space=pltpu.VMEM)],
        out_specs=pl.BlockSpec(memory_space=pltpu.VMEM),
        scratch_shapes=[pltpu.VMEM((orient,) + rows.shape, jnp.float32)]
        + [pltpu.SemaphoreType.DMA((orient,))] * 2,
        compiler_params=pltpu.CompilerParams(
            collective_id=1, has_side_effects=True, vmem_limit_bytes=16 * 2**20
        ),
    )(rows)
    return stats.reshape(orient, 2, -1)[:, :, :count]


def shards(groups, orient, images, templates, index, interp, inv_noise):
    side = inv_noise.shape[0]
    volume_rows = side * side
    noise_flat = inv_noise.reshape(-1)
    index_t, interp_t = index.T, interp.T
    gathered = lax.all_gather(images, "orient", axis=0, tiled=True)
    places = jnp.concatenate([index.astype(jnp.float32), interp], axis=1)
    gathered, places = lax.optimization_barrier((gathered, places))
    places_all = lax.all_gather(places, "orient", axis=0, tiled=True)
    tpl_f = templates.astype(jnp.float32)
    weighted = (tpl_f * noise_flat[None, :]).astype(jnp.bfloat16)
    tnorm = 0.5 * jnp.sum(tpl_f * tpl_f * noise_flat[None, :], axis=1)
    scores = (
        lax.dot_general(
            weighted, gathered, (((1,), (1,)), ((), ())), preferred_element_type=jnp.float32
        )
        - tnorm[:, None]
    )
    peak_own = jnp.max(scores, axis=0)
    expo = jnp.exp(scores - peak_own[None, :])
    stats = gather_stats(jnp.stack([peak_own, jnp.sum(expo, axis=0)]), orient)
    peak = jnp.max(stats[:, 0], axis=0)
    total = jnp.sum(stats[:, 1] * jnp.exp(stats[:, 0] - peak[None, :]), axis=0)
    posterior = expo * (jnp.exp(peak_own - peak) / total)[None, :]
    mass = jnp.sum(posterior, axis=1)
    data_vol = insert_data(
        posterior.astype(jnp.bfloat16), gathered, interp_t, index_t, volume_rows
    )
    rows = volume_rows // (groups * orient)
    first = (lax.axis_index("dp") * orient + lax.axis_index("orient")) * rows
    return reduce_rows(
        data_vol,
        mass,
        places_all[:, :side].astype(jnp.int32).T - first,
        places_all[:, side:].T,
        inv_noise,
        groups,
        orient,
    )


def solution(mesh):
    placed = (
        P(("dp", "orient"), None),
        P("orient", None),
        P("orient", None),
        P("orient", None),
        P(),
    )
    return jax.shard_map(
        functools.partial(shards, mesh.shape["dp"], mesh.shape["orient"]),
        mesh=mesh,
        in_specs=placed,
        out_specs=(P(("dp", "orient"), None), P(("dp", "orient"), None)),
        check_vma=False,
    )
```
